32 devices in a mesh: dp: 8 (over z, y), seq: 4 (over x, core).
Axes of the slice: x: 2, y: 2, z: 4, core: 2. Of those that a mesh axis runs over, the one named last changes fastest.
Arguments:
- tokens: bfloat16 [4096, 2880], P(('dp', 'seq')), may hold values from -6 to 6
- norm_gain: bfloat16 [2880], replicated, may hold values from 0.5 to 1.5
- router_weight: bfloat16 [2880, 16], replicated, may hold values from -0.109375 to 0.109375
- expert_ids: int32 [4096, 4], P(('dp', 'seq')), may hold values from 0 to 15, all different within a row; in each aligned block of 128 rows (0 to 127, 128 to 255, ...) at most 36 rows name the same one
- gate_up_words: int32 [32, 1440, 1440], P(('dp', 'seq')), may hold values from 0 to 255
- gate_up_scales: int32 [32, 90, 1440], P(('dp', 'seq')), may hold values from 119 to 121
- down_words: int32 [32, 720, 1440], P(('dp', 'seq')), may hold values from 0 to 255
- down_scales: int32 [32, 720, 90], P(('dp', 'seq')), may hold values from 119 to 121
- cotangent: bfloat16 [4096, 2880], P(('dp', 'seq')), may hold values from -6 to 6
Outputs:
- mixed: bfloat16 [4096, 2880], P(('dp', 'seq'))
- token_grad: bfloat16 [4096, 2880], P(('dp', 'seq'))
The draws below stay inside these ranges and needn't reach their ends.
Inputs may be any that keep to these rules, and one draw needn't show every extreme that they name: `expert_ids`: in each device's aligned block of 128 tokens no expert is named more than 36 times, a bound that some block reaches.
All inputs are finite; a program needn't handle non-finite values.
Results may differ from the reference program's by a relative error of at most 0.0029.
Values may be sent and summed in bfloat16 or wider, within the bound.
A program may use at most 192 MiB of HBM per device.

```python
import math
import jax
import jax.numpy as jnp
import numpy as np
from jax import lax

D = 2880
HIDDEN_SIZE = 1440
TOP = 4
TOK_DEV = 128
HALF = 720
EXPERTS = 16
CAP = 36
TOKENS = 4096
N_DP = 8
N_SEQ = 4


def plant(entries, own_key, least, high):
    longest = entries.shape.index(max(entries.shape))
    spots = []
    for shift in (0, 1):
        where = [jax.random.randint(jax.random.fold_in(own_key, axis), (), 0, length) for axis, length in enumerate(entries.shape)]
        where[longest] = (where[longest] + shift) % entries.shape[longest]
        spots.append(tuple(where))
    return entries.at[spots[0]].set(least).at[spots[1]].set(high)


def levels(stream_key, extent, cuts, smallest, high):
    def one(position, blocks):
        steps = jax.random.uniform(jax.random.fold_in(jax.random.fold_in(stream_key, 6), position), (blocks,), jnp.float32, smallest / len(cuts), high / len(cuts))
        return jnp.repeat(jnp.exp(steps), extent[position] // blocks).reshape((-1,) + (1,) * (len(extent) - position - 1))

    level = one(*cuts[0])
    for cut in cuts[1:]:
        level = level * one(*cut)
    return level


def assign_block(stream_key, own, number, rows, count, top, reach, slope):
    sequence = jax.random.permutation(stream_key, count)
    packed, usual = shares(count, rows * top, reach, slope, True), shares(count, rows * top, reach, slope, False)
    places = jnp.arange(count)

    def named(tallies, turn):
        used = int((tallies > 0).sum())
        fixed = max(1, used // 4)
        shifted = fixed + (places - fixed + turn * (used - fixed)) % max(1, count - fixed)
        return jnp.zeros((count,), jnp.int32).at[sequence[jnp.where(places < fixed, places, shifted)]].set(jnp.asarray(tallies, jnp.int32))

    tallies = jnp.where(number % 4 == 0, named(packed, number // 4), named(usual, number - number // 4 - 1))
    mixed = jax.random.permutation(jax.random.fold_in(own, 3), count)
    giver, receiver = mixed[0:count // 2 * 2:2], mixed[1:count // 2 * 2:2]
    margin = jnp.minimum(tallies[giver] - 1, reach - tallies[receiver]) // 2
    margin = jnp.where((giver == sequence[0]) | (receiver == sequence[0]) | (tallies[receiver] == 0), 0, jnp.maximum(margin, 0))
    shifted = jax.random.randint(jax.random.fold_in(own, 4), (count // 2,), 0, 1 << 20) % (margin + 1)
    tallies = tallies.at[giver].add(-shifted).at[receiver].add(shifted)
    items = jnp.searchsorted(jnp.cumsum(tallies), jnp.arange(rows * top), side="right").astype(jnp.int32)
    listing = items.reshape(top, rows).T
    listing = listing[jax.random.permutation(jax.random.fold_in(own, 1), rows)]
    turn = jax.random.randint(jax.random.fold_in(own, 2), (rows, 1), 0, top)
    return jnp.take_along_axis(listing, (jnp.arange(top)[None, :] + turn) % top, axis=1)


def shares(amount, total, most, lean, full):
    loads = [(1 << 20) // math.isqrt(grade ** lean) + 1 for grade in range(1, amount + 1)]
    largest = most if full else min(most, max(-(-total // amount), total * loads[0] // sum(loads)))
    least = 1 if total - largest >= amount - 1 else 0
    counts, rest = [largest] + [least] * (amount - 1), total - largest - least * (amount - 1)
    while rest > 0:
        candidates = [i for i in range(1, amount) if counts[i] < largest] or [i for i in range(1, amount) if counts[i] < most]
        whole, remaining = sum([loads[i] for i in candidates]), rest
        for i in candidates:
            addition = min(most - counts[i], max(1, remaining * loads[i] // whole), rest)
            counts[i] = counts[i] + addition
            rest = rest - addition
    return np.array(counts)


def normal_values(stream_key, extent, width, bound, pieces=(), kind=jnp.bfloat16):
    result = width * jax.random.normal(stream_key, extent, jnp.float32)
    if pieces:
        result = result * levels(stream_key, extent, pieces, -0.22, 0.18)
    return jnp.clip(result, -bound, bound).astype(kind)


def setup_inputs(seed: int = 0) -> dict:
    keys = jax.random.split(jax.random.key(seed), 10)
    tokens = normal_values(keys[0], (TOKENS, D), 1.0, 6.0, ((0, 32),))
    norm_gain = jnp.clip(1.0 + 0.1 * jax.random.normal(keys[1], (D,), jnp.float32), 0.5, 1.5).astype(jnp.bfloat16)
    router_weight = normal_values(keys[2], (D, EXPERTS), D ** -0.5, 0.109375)
    expert_ids_keys = jax.random.split(jax.random.fold_in(keys[3], 1), TOKENS // TOK_DEV)
    expert_ids_turns = jax.random.permutation(jax.random.fold_in(keys[3], 3), TOKENS // TOK_DEV)
    expert_ids = jax.vmap(lambda own, number: assign_block(jax.random.fold_in(keys[3], 2), own, number, TOK_DEV, EXPERTS, TOP, CAP, 2))(expert_ids_keys, expert_ids_turns).reshape((TOKENS, TOP))
    gate_up_words = plant(jax.random.randint(keys[4], (2 * EXPERTS, D // 2, HIDDEN_SIZE), 0, 256), jax.random.fold_in(keys[4], 1), 0, 255).astype(jnp.int32)
    gate_up_scales = plant(jax.random.randint(keys[5], (2 * EXPERTS, D // 32, HIDDEN_SIZE), 119, 122), jax.random.fold_in(keys[5], 1), 119, 121).astype(jnp.int32)
    down_words = plant(jax.random.randint(keys[6], (2 * EXPERTS, HALF, D // 2), 0, 256), jax.random.fold_in(keys[6], 1), 0, 255).astype(jnp.int32)
    down_scales = plant(jax.random.randint(keys[7], (2 * EXPERTS, HALF, D // 32), 119, 122), jax.random.fold_in(keys[7], 1), 119, 121).astype(jnp.int32)
    cotangent = normal_values(keys[8], (TOKENS, D), 1.0, 6.0, ((0, 32),))
    return dict(tokens=tokens, norm_gain=norm_gain, router_weight=router_weight, expert_ids=expert_ids, gate_up_words=gate_up_words, gate_up_scales=gate_up_scales, down_words=down_words, down_scales=down_scales, cotangent=cotangent)


glu_slope = 1.702
norm_epsilon = 1e-05

def small_float(code_values):
    sign_part = code_values // 8
    level_code = code_values % 8
    exponent = level_code // 2
    mantissa = (level_code % 2).astype(jnp.float32)
    scaled = jnp.exp2((exponent - 1).astype(jnp.float32)) * (1.0 + 0.5 * mantissa)
    magnitude = jnp.where(exponent == 0, 0.5 * mantissa, scaled)
    return jnp.where(sign_part == 1, -magnitude, magnitude)

def unpack_rows(code_words, scale_codes):
    groups = scale_codes.shape[0]
    columns = code_words.shape[1]
    factor = jnp.exp2((scale_codes - 127).astype(jnp.float32))[:, None, :]
    shaped = code_words.reshape(groups, -1, columns)
    low_vals = (small_float(shaped % 16) * factor).astype(jnp.bfloat16)
    high_vals = (small_float(shaped // 16) * factor).astype(jnp.bfloat16)
    return jnp.stack([low_vals, high_vals], axis=2).reshape(-1, columns)

def unpack_cols(code_words, scale_codes):
    lines = code_words.shape[0]
    groups = scale_codes.shape[1]
    factor = jnp.exp2((scale_codes - 127).astype(jnp.float32))[:, :, None]
    shaped = code_words.reshape(lines, groups, -1)
    low_vals = (small_float(shaped % 16) * factor).astype(jnp.bfloat16)
    high_vals = (small_float(shaped // 16) * factor).astype(jnp.bfloat16)
    return jnp.stack([low_vals, high_vals], axis=3).reshape(lines, -1)

def expert_half(rows_in, grads_in, gate_up, down_proj):
    half_units = down_proj.shape[0]
    pre_act = jnp.dot(rows_in, gate_up, preferred_element_type=jnp.float32)
    gate_pre = pre_act[:, :half_units]
    up_pre = pre_act[:, half_units:]
    sig_gate = jax.nn.sigmoid(glu_slope * gate_pre)
    glu_gate = gate_pre * sig_gate
    active = (glu_gate * (up_pre + 1.0)).astype(jnp.bfloat16)
    part_out = jnp.dot(active, down_proj, preferred_element_type=jnp.float32).astype(jnp.bfloat16)
    back_act = lax.dot_general(grads_in, down_proj, (((1,), (1,)), ((), ())), preferred_element_type=jnp.float32)
    slope_term = sig_gate + glu_slope * glu_gate * (1.0 - sig_gate)
    grad_pre = jnp.concatenate([back_act * (up_pre + 1.0) * slope_term, back_act * glu_gate], axis=1).astype(jnp.bfloat16)
    part_back = lax.dot_general(grad_pre, gate_up, (((1,), (1,)), ((), ())), preferred_element_type=jnp.float32).astype(jnp.bfloat16)
    return (part_out, part_back)

def reference(tokens, norm_gain, router_weight, expert_ids, gate_up_words, gate_up_scales, down_words, down_scales, cotangent):
    device_total = N_DP * N_SEQ
    tok_f = tokens.astype(jnp.float32)
    cot_f = cotangent.astype(jnp.float32)
    gain_f = norm_gain.astype(jnp.float32)
    inv_rms = lax.rsqrt(lax.optimization_barrier(jnp.mean(tok_f * tok_f, axis=1, keepdims=True)) + norm_epsilon)
    normed = (tok_f * inv_rms * gain_f).astype(jnp.bfloat16)
    logits = jnp.dot(normed, router_weight, preferred_element_type=jnp.float32)
    one_hot = expert_ids[:, :, None] == jnp.arange(EXPERTS, dtype=jnp.int32)
    picked = lax.optimization_barrier(jnp.sum(jnp.where(one_hot, logits[:, None, :], 0.0), axis=2))
    raised = jnp.exp(picked)
    probs = raised / lax.optimization_barrier(jnp.sum(raised, axis=1, keepdims=True))
    flat_probs = probs.reshape(-1)
    pair_count = TOKENS * TOP
    flat_hot = one_hot.reshape(device_total, TOK_DEV * TOP, EXPERTS).astype(jnp.int32)
    running = jnp.cumsum(flat_hot, axis=1)
    slot_of = (lax.optimization_barrier(jnp.sum(running * flat_hot, axis=2)) - 1).reshape(-1).astype(jnp.int32)
    pair_index = jnp.arange(pair_count, dtype=jnp.int32)
    device_of = pair_index // (TOK_DEV * TOP)
    flat_ids = expert_ids.reshape(-1).astype(jnp.int32)
    table = jnp.full((EXPERTS, device_total * CAP), pair_count, jnp.int32)
    table = table.at[flat_ids, device_of * CAP + slot_of].set(pair_index)

    def per_expert(carried, expert):
        mixed_acc, back_acc, dprob_acc = carried
        slot_pairs = table[expert]
        filled = slot_pairs < pair_count
        safe_pair = jnp.minimum(slot_pairs, pair_count - 1)
        safe_token = safe_pair // TOP
        rows_in = jnp.where(filled[:, None], normed[safe_token], 0)
        grads_in = jnp.where(filled[:, None], (flat_probs[safe_pair][:, None] * cot_f[safe_token]).astype(jnp.bfloat16), 0)
        total_out = jnp.zeros((slot_pairs.shape[0], D), jnp.float32)
        total_back = jnp.zeros((slot_pairs.shape[0], D), jnp.float32)
        for half_index in range(2):
            which = 2 * expert + half_index
            gate_up = unpack_rows(lax.dynamic_index_in_dim(gate_up_words, which, 0, keepdims=False), lax.dynamic_index_in_dim(gate_up_scales, which, 0, keepdims=False))
            down_proj = unpack_cols(lax.dynamic_index_in_dim(down_words, which, 0, keepdims=False), lax.dynamic_index_in_dim(down_scales, which, 0, keepdims=False))
            part_out, part_back = expert_half(rows_in, grads_in, gate_up, down_proj)
            total_out = total_out + part_out.astype(jnp.float32)
            total_back = total_back + part_back.astype(jnp.float32)
        weight = jnp.where(filled, flat_probs[safe_pair], 0.0)
        mixed_acc = mixed_acc.at[safe_token].add(weight[:, None] * total_out)
        back_acc = back_acc.at[safe_token].add(jnp.where(filled[:, None], total_back, 0.0))
        dprob_acc = dprob_acc.at[safe_pair].add(jnp.where(filled, lax.optimization_barrier(jnp.sum(cot_f[safe_token] * total_out, axis=1)), 0.0))
        return ((mixed_acc, back_acc, dprob_acc), None)
    start = (jnp.zeros((TOKENS, D), jnp.float32), jnp.zeros((TOKENS, D), jnp.float32), jnp.zeros((pair_count,), jnp.float32))
    (mixed_acc, back_acc, dprob_acc), _ = lax.scan(per_expert, start, jnp.arange(EXPERTS, dtype=jnp.int32))
    mixed = (tok_f + mixed_acc).astype(jnp.bfloat16)
    dprob = dprob_acc.reshape(TOKENS, TOP)
    dpicked = probs * (dprob - lax.optimization_barrier(jnp.sum(probs * dprob, axis=1, keepdims=True)))
    dlogits = lax.optimization_barrier(jnp.sum(jnp.where(one_hot, dpicked[:, :, None], 0.0), axis=1))
    dnormed = jnp.dot(dlogits, router_weight.astype(jnp.float32).T, precision=lax.Precision.HIGHEST) + back_acc
    gain_grad = gain_f * dnormed
    token_grad = cot_f + inv_rms * gain_grad - tok_f * (inv_rms * inv_rms * inv_rms) * lax.optimization_barrier(jnp.mean(gain_grad * tok_f, axis=1, keepdims=True))
    return (mixed, token_grad.astype(jnp.bfloat16))
```

```python
import jax
import jax.numpy as jnp
from jax import lax
from jax.experimental import pallas as pl
from jax.experimental.pallas import tpu as pltpu
from jax.sharding import PartitionSpec as P

glu_slope = 1.702
norm_epsilon = 1e-05


def small_float(codes):
    level = (codes & 7).astype(jnp.float32)
    magnitude = jnp.maximum(jnp.maximum(0.5 * level, level - 2.0), 2.0 * level - 8.0)
    return jnp.where(codes >= 8, -magnitude, magnitude)


def decode_kernel(words_ref, factor_ref, out_ref, wide_ref):
    columns = words_ref.shape[1]
    for group in range(factor_ref.shape[1]):
        for number, start in enumerate(range(0, columns, 128)):
            lanes = min(128, columns - start)
            words = words_ref[pl.ds(16 * group, 16), pl.ds(start, lanes)]
            factor = factor_ref[0, pl.ds(group, 1), pl.ds(start, lanes)]
            low_vals = small_float(words & 15) * factor
            high_vals = small_float(words >> 4) * factor
            if lanes < 128:
                rest = jnp.zeros((16, 128 - lanes), jnp.float32)
                low_vals = jnp.concatenate([low_vals, rest], axis=1)
                high_vals = jnp.concatenate([high_vals, rest], axis=1)
            slot = wide_ref.at[number]
            slot[pl.ds(0, 16, stride=2), :] = low_vals
            slot[pl.ds(1, 16, stride=2), :] = high_vals
            out_ref[pl.ds(32 * group, 32), pl.ds(start, lanes)] = slot[:, :lanes].astype(jnp.bfloat16)


def unpack_rows(code_words, scale_codes):
    groups, columns = scale_codes.shape
    at_once = 10 if groups % 10 == 0 else 1
    factor = jnp.exp2((scale_codes - 127).astype(jnp.float32))
    return pl.pallas_call(
        decode_kernel,
        grid=(groups // at_once,),
        in_specs=[
            pl.BlockSpec((16 * at_once, columns), lambda step: (step, 0)),
            pl.BlockSpec((1, at_once, columns), lambda step: (step, 0, 0)),
        ],
        out_specs=pl.BlockSpec((32 * at_once, columns), lambda step: (step, 0)),
        out_shape=jax.ShapeDtypeStruct((32 * groups, columns), jnp.bfloat16),
        scratch_shapes=[pltpu.VMEM((-(-columns // 128), 32, 128), jnp.float32)],
        compiler_params=pltpu.CompilerParams(vmem_limit_bytes=24 * 1024 * 1024),
        cost_estimate=pl.CostEstimate(
            flops=16 * 32 * groups * columns, bytes_accessed=8 * 16 * groups * columns, transcendentals=0
        ),
    )(code_words, factor.reshape(groups // at_once, at_once, columns))


def expert_half(rows_in, grads_in, gate_up, down_turned):
    half_units = down_turned.shape[1]
    pre_act = jnp.dot(rows_in, gate_up, preferred_element_type=jnp.float32)
    gate_pre = pre_act[:, :half_units]
    up_pre = pre_act[:, half_units:]
    sig_gate = jax.nn.sigmoid(glu_slope * gate_pre)
    glu_gate = gate_pre * sig_gate
    active = (glu_gate * (up_pre + 1.0)).astype(jnp.bfloat16)
    part_out = lax.reduce_precision(
        lax.dot_general(
            active, down_turned, (((1,), (1,)), ((), ())), preferred_element_type=jnp.float32
        ),
        8,
        7,
    ).astype(jnp.bfloat16)
    back_act = jnp.dot(grads_in, down_turned, preferred_element_type=jnp.float32)
    slope_term = sig_gate + glu_slope * glu_gate * (1.0 - sig_gate)
    grad_pre = jnp.concatenate(
        [back_act * (up_pre + 1.0) * slope_term, back_act * glu_gate], axis=1
    ).astype(jnp.bfloat16)
    part_back = lax.reduce_precision(
        lax.dot_general(
            grad_pre, gate_up, (((1,), (1,)), ((), ())), preferred_element_type=jnp.float32
        ),
        8,
        7,
    ).astype(jnp.bfloat16)
    return (part_out, part_back)


def shards(
    tokens,
    norm_gain,
    router_weight,
    expert_ids,
    gate_up_words,
    gate_up_scales,
    down_words,
    down_scales,
    cotangent,
):
    tok_count, width = tokens.shape
    top_count = expert_ids.shape[1]
    dp_count = lax.axis_size("dp")
    seq_count = lax.axis_size("seq")
    devices = dp_count * seq_count
    experts = devices // 2
    capacity = -(-(tok_count * top_count * 9 // (8 * experts)) // 8) * 8
    tok_f = tokens.astype(jnp.float32)
    cot_f = cotangent.astype(jnp.float32)
    gain_f = norm_gain.astype(jnp.float32)
    inv_rms = lax.rsqrt(jnp.mean(tok_f * tok_f, axis=1, keepdims=True) + norm_epsilon)
    normed = (tok_f * inv_rms * gain_f).astype(jnp.bfloat16)
    logits = jnp.dot(normed, router_weight, preferred_element_type=jnp.float32)
    expert_cols = lax.broadcasted_iota(jnp.int32, (tok_count, top_count, experts), 2)
    one_hot = expert_ids[:, :, None] == expert_cols
    picked = jnp.sum(jnp.where(one_hot, logits[:, None, :], 0.0), axis=2)
    raised = jnp.exp(picked)
    probs = raised / jnp.sum(raised, axis=1, keepdims=True)

    slots = experts * capacity
    named = jnp.any(one_hot, axis=1)
    earlier = (
        lax.broadcasted_iota(jnp.int32, (tok_count, tok_count), 1)
        < lax.broadcasted_iota(jnp.int32, (tok_count, tok_count), 0)
    )
    before = jnp.dot(
        earlier.astype(jnp.bfloat16), named.astype(jnp.bfloat16), preferred_element_type=jnp.float32
    )
    slot_of = jnp.sum(jnp.where(one_hot, before[:, None, :], 0.0), axis=2).astype(jnp.int32)
    target = expert_ids * capacity + slot_of
    slot_cols = lax.broadcasted_iota(jnp.int32, (tok_count, slots), 1)
    place = jnp.zeros((tok_count, slots), jnp.bool_)
    weight = jnp.zeros((tok_count, slots), jnp.float32)
    for k in range(top_count):
        hit = target[:, k : k + 1] == slot_cols
        place = place | hit
        weight = jnp.where(hit, probs[:, k : k + 1], weight)
    place_b = place.astype(jnp.bfloat16)
    to_slots = (((0,), (0,)), ((), ()))
    slot_rows = lax.dot_general(
        place_b, normed, to_slots, preferred_element_type=jnp.float32
    ).astype(jnp.bfloat16)
    slot_cot = lax.dot_general(place_b, cotangent, to_slots, preferred_element_type=jnp.float32)
    slot_prob = jnp.sum(weight, axis=0)[:, None]
    slot_grads = lax.reduce_precision(slot_prob * slot_cot, 8, 7).astype(jnp.bfloat16)
    gate_up = unpack_rows(gate_up_words[0], gate_up_scales[0])
    down_turned = unpack_rows(down_words[0].T, down_scales[0].T)

    both = jnp.stack(
        [
            slot_rows.reshape(experts, capacity, width),
            slot_grads.reshape(experts, capacity, width),
        ],
        axis=1,
    ).reshape(devices, capacity, width)
    mine = lax.all_to_all(both, ("dp", "seq"), split_axis=0, concat_axis=0, tiled=True)
    mine = mine.reshape(devices * capacity, width)
    swap = [(i, i ^ 1) for i in range(seq_count)]
    other = lax.ppermute(mine, "seq", swap)
    first = lax.rem(lax.axis_index("seq"), 2) == 0
    rows_in = jnp.where(first, mine, other)
    grads_in = jnp.where(first, other, mine)
    part_out, part_back = expert_half(rows_in, grads_in, gate_up, down_turned)
    back_out = lax.all_to_all(
        part_out.reshape(devices, capacity, width), ("dp", "seq"), split_axis=0, concat_axis=0, tiled=True
    ).reshape(2 * slots, width)
    back_grad = lax.all_to_all(
        part_back.reshape(devices, capacity, width), ("dp", "seq"), split_axis=0, concat_axis=0, tiled=True
    ).reshape(2 * slots, width)

    half_target = expert_ids * (2 * capacity) + slot_of
    half_cols = lax.broadcasted_iota(jnp.int32, (tok_count, 2 * slots), 1)
    hits = []
    place_half = jnp.zeros((tok_count, 2 * slots), jnp.bool_)
    weight_half = jnp.zeros((tok_count, 2 * slots), jnp.float32)
    for k in range(top_count):
        start = half_target[:, k : k + 1]
        hit = (start == half_cols) | (start + capacity == half_cols)
        hits.append(hit)
        place_half = place_half | hit
        weight_half = jnp.where(hit, probs[:, k : k + 1], weight_half)
    weight_high = lax.reduce_precision(weight_half, 8, 7)
    weight_low = weight_half - weight_high
    mix = jnp.dot(
        weight_high.astype(jnp.bfloat16), back_out, preferred_element_type=jnp.float32
    ) + jnp.dot(weight_low.astype(jnp.bfloat16), back_out, preferred_element_type=jnp.float32)
    mixed = (tok_f + mix).astype(jnp.bfloat16)
    dots = lax.dot_general(
        cotangent, back_out, (((1,), (1,)), ((), ())), preferred_element_type=jnp.float32
    )
    dprob = jnp.stack([jnp.sum(jnp.where(hit, dots, 0.0), axis=1) for hit in hits], axis=1)
    dpicked = probs * (dprob - jnp.sum(probs * dprob, axis=1, keepdims=True))
    dlogits = jnp.sum(jnp.where(one_hot, dpicked[:, :, None], 0.0), axis=1)
    dnormed = jnp.dot(
        dlogits, router_weight.astype(jnp.float32).T, precision=lax.Precision.HIGHEST
    ) + jnp.dot(
        place_half.astype(jnp.bfloat16), back_grad, preferred_element_type=jnp.float32
    )
    gain_grad = gain_f * dnormed
    token_grad = (
        cot_f
        + inv_rms * gain_grad
        - tok_f * (inv_rms * inv_rms * inv_rms) * jnp.mean(gain_grad * tok_f, axis=1, keepdims=True)
    )
    return (mixed, token_grad.astype(jnp.bfloat16))


def solution(mesh):
    in_specs = (
        P(("dp", "seq"), None),
        P(),
        P(),
        P(("dp", "seq"), None),
        P(("dp", "seq"), None, None),
        P(("dp", "seq"), None, None),
        P(("dp", "seq"), None, None),
        P(("dp", "seq"), None, None),
        P(("dp", "seq"), None),
    )
    out_specs = (P(("dp", "seq"), None), P(("dp", "seq"), None))
    return jax.shard_map(shards, mesh=mesh, in_specs=in_specs, out_specs=out_specs, check_vma=False)
```
